32 devices in a mesh: row: 8 (over z, y), col: 4 (over x, core).
Axes of the slice: x: 2, y: 2, z: 4, core: 2. Of those that a mesh axis runs over, the one named last changes fastest.
Arguments:
- tile_values: bfloat16 [64, 192, 128, 128], P('row', 'col'), may hold values from -0.078125 to 0.078125
- block_cols: int32 [64, 192], P('row', 'col'), may hold values from 0 to 4096, as said below
- primal_start: float32 [524288], P('col'), may hold values from -6 to 6
- dual_start: float32 [8192], P('row'), may hold values from -6 to 6
- cost_vector: float32 [524288], P('col'), may hold values from -6 to 6
- lower_bound: float32 [524288], P('col'), may hold values from -1 to -0.1
- upper_bound: float32 [524288], P('col'), may hold values from 0.1 to 1
- var_kinds: int32 [524288], P('col'), may hold values from 0 to 2
- right_side: float32 [8192], P('row'), may hold values from -6 to 6
- row_kinds: int32 [8192], P('row'), may hold values from 0 to 1
Outputs:
- primal_final: float32 [524288], P('col')
- dual_final: float32 [8192], P('row')
The draws below stay inside these ranges and needn't reach their ends.
Inputs may be any that keep to these rules, and one draw needn't show every extreme that they name: `block_cols`: slots holding 4096 are empty; in each row band the live slots of index c of col come first and name column blocks c * 1024 to c * 1024 + 1023; one index of col holds all 48 slots live for some band.
All inputs are finite; a program needn't handle non-finite values.
Results may differ from the reference program's by a relative error of at most 0.002.
Values may be sent and summed in bfloat16 or wider, within the bound.
A program may use at most 64 MiB of HBM per device.

```python
import jax
import jax.numpy as jnp
from jax import lax

BS = 128
NB_DEV = 1024
CAP_DEV = 48
NB = 4096
MB = 64
CAP = 192
N = 524288
M = 8192
N_COL = 4


def draw_block_cols(key, part):
    keys = jax.random.split(key, 5)
    band_index = jnp.arange(MB)[:, None, None]
    weight = jax.random.randint(keys[0], (MB, 1, 1), 1, 4)
    heavy_band = jax.random.randint(keys[1], (), 0, MB)
    light_band = (heavy_band + 1) % MB
    weight = jnp.where(band_index == heavy_band, 3, weight)
    weight = jnp.where(band_index == light_band, 1, weight)
    jitter = jax.random.randint(keys[2], (MB, N_COL, 1), 0, CAP_DEV // 6 + 1)
    full_dev = jax.random.randint(keys[3], (MB, 1, 1), 0, N_COL)
    jitter = jnp.where(jnp.arange(N_COL)[None, :, None] == full_dev, 0, jitter)
    live_count = weight * (CAP_DEV // 3) - jitter
    slot_index = jnp.arange(CAP_DEV)[None, None, :]
    shard_base = jnp.arange(N_COL)[None, :, None] * NB_DEV
    column_ids = jax.random.randint(keys[4], (MB, N_COL, CAP_DEV), 0, NB_DEV) + shard_base
    chosen = jnp.where(slot_index < live_count, column_ids, NB)
    return chosen.reshape(MB, N_COL * CAP_DEV).astype(jnp.int32)


def plant(values, rng, smallest, high):
    shape = values.shape
    index_at = [jax.random.randint(jax.random.fold_in(rng, axis), (), 0, shape[axis]) for axis in range(len(shape))]
    values = values.at[tuple(index_at)].set(smallest)
    longest = shape.index(max(shape))
    index_at[longest] = (index_at[longest] + 1) % shape[longest]
    return values.at[tuple(index_at)].set(high)


def steps_of(own_key, extent, cuts, smallest, top_value):
    level = 1.0
    for position, parts in cuts:
        draws = jax.random.uniform(jax.random.fold_in(jax.random.fold_in(own_key, 6), position), (parts,), jnp.float32, smallest / len(cuts), top_value / len(cuts))
        level = level * jnp.repeat(jnp.exp(draws), extent[position] // parts).reshape((-1,) + (1,) * (len(extent) - 1 - position))
    return level


def normal_values(own_key, dims, width, reach, cuts=(), held_as=jnp.bfloat16):
    result = width * jax.random.normal(own_key, dims, jnp.float32)
    if cuts:
        result = result * steps_of(own_key, dims, cuts, -0.22, 0.18)
    return jnp.clip(result, -reach, reach).astype(held_as)


def setup_inputs(seed: int = 0) -> dict:
    seeds = jax.random.split(jax.random.key(seed), 11)
    return {
        "tile_values": normal_values(seeds[0], (MB, CAP, BS, BS), (32 * CAP) ** -0.5, 0.078125, ((0, 8), (1, 4))),
        "block_cols": draw_block_cols(jax.random.fold_in(seeds[10], 71), 0),
        "primal_start": normal_values(seeds[2], (N,), 1.0, 6.0, ((0, 4),), jnp.float32),
        "dual_start": normal_values(seeds[3], (M,), 1.0, 6.0, ((0, 8),), jnp.float32),
        "cost_vector": normal_values(seeds[4], (N,), 1.0, 6.0, ((0, 4),), jnp.float32),
        "lower_bound": jnp.clip(-1.0 + 0.9 * jax.random.uniform(seeds[5], (N,), jnp.float32) ** steps_of(seeds[5], (N,), ((0, 4),), -0.2, 0.2), -1.0, -0.1),
        "upper_bound": jnp.clip(0.1 + 0.9 * jax.random.uniform(seeds[6], (N,), jnp.float32) ** steps_of(seeds[6], (N,), ((0, 4),), -0.2, 0.2), 0.1, 1.0),
        "var_kinds": plant(jax.random.randint(seeds[7], (N,), 0, 3), jax.random.fold_in(seeds[7], 1), 0, 2).astype(jnp.int32),
        "right_side": normal_values(seeds[8], (M,), 1.0, 6.0, ((0, 8),), jnp.float32),
        "row_kinds": plant(jax.random.randint(seeds[9], (M,), 0, 2), jax.random.fold_in(seeds[9], 1), 0, 1).astype(jnp.int32),
    }


step_size = 0.8
epsilon = 1e-06

def project_primal(vector, lower_bound, upper_bound, var_kinds):
    raised = jnp.where(var_kinds >= 1, jnp.maximum(vector, lower_bound), vector)
    return jnp.where(var_kinds == 2, jnp.minimum(raised, upper_bound), raised)

def project_dual(vector, row_kinds):
    return jnp.where(row_kinds == 1, jnp.maximum(vector, 0.0), vector)

def forward_product(tile_values, block_cols, extrapolated):
    blocks = jnp.concatenate([extrapolated.reshape(NB, BS), jnp.zeros((1, BS), extrapolated.dtype)], axis=0)

    def one_band(band_pair):
        band_tiles, band_cols = band_pair
        picked = blocks[band_cols].astype(jnp.float32)
        return jnp.einsum('sij,sj->i', band_tiles.astype(jnp.float32), picked)
    return lax.map(one_band, (tile_values, block_cols)).reshape(-1)

def transpose_product(tile_values, block_cols, dual_half):
    dual_bands = dual_half.reshape(MB, BS)

    def one_band(running, triple):
        band_tiles, band_cols, dual_band = triple
        contrib = jnp.einsum('sij,i->sj', band_tiles.astype(jnp.float32), dual_band.astype(jnp.float32))
        return (running.at[band_cols].add(contrib), None)
    summed, _ = lax.scan(one_band, jnp.zeros((NB + 1, BS), jnp.float32), (tile_values, block_cols, dual_bands))
    return summed[:NB].reshape(-1)

def reference(tile_values, block_cols, primal_start, dual_start, cost_vector, lower_bound, upper_bound, var_kinds, right_side, row_kinds):

    def iterate(primal, dual, primal_weight):
        primal_step = step_size / primal_weight
        dual_step = step_size * primal_weight
        col_product = transpose_product(tile_values, block_cols, dual.astype(jnp.bfloat16))
        primal_next = project_primal(primal - primal_step * (cost_vector - col_product), lower_bound, upper_bound, var_kinds)
        extrapolated = (2.0 * primal_next - primal).astype(jnp.bfloat16)
        row_product = forward_product(tile_values, block_cols, extrapolated)
        dual_next = project_dual(dual + dual_step * (right_side - row_product), row_kinds)
        return (primal_next, dual_next)
    primal_one, dual_one = iterate(primal_start, dual_start, 1.0)
    primal_moved = jnp.sum((primal_one - primal_start) ** 2)
    dual_moved = jnp.sum((dual_one - dual_start) ** 2)
    primal_weight = jnp.sqrt(jnp.sqrt((dual_moved + epsilon) / (primal_moved + epsilon)))
    primal_final, dual_final = iterate(primal_one, dual_one, primal_weight)
    return (primal_final, dual_final)
```

```python
import functools

import jax
import jax.numpy as jnp
from jax import lax
from jax.experimental import pallas as pl
from jax.experimental.pallas import tpu as pltpu
from jax.sharding import PartitionSpec as P

step_size = 0.8
epsilon = 1e-06
OUTER = 4
GROUP = 16
CHUNKS = 2
MESH_ID = pl.DeviceIdType.MESH


def project_primal(vector, lower_bound, upper_bound, var_kinds):
    raised = jnp.where(var_kinds >= 1, jnp.maximum(vector, lower_bound), vector)
    return jnp.where(var_kinds == 2, jnp.minimum(raised, upper_bound), raised)


def project_dual(vector, row_kinds):
    return jnp.where(row_kinds == 1, jnp.maximum(vector, 0.0), vector)


def kernel(
    rows, cols, bands, slots, width, blocks,
    tiles_hbm, ids_row, ids_col, primal_hbm, cost_hbm, lower_hbm, upper_hbm, kinds_hbm,
    dual_ref, right_ref, row_kinds_ref,
    primal_out, dual_out,
    tiles, primal, cost, lower, upper, kinds, result,
    hot, hot_own, xbar, picked, contrib, ids_all, partial, moved_dual,
    tile_sem, in_sem, out_sem,
    own_send, fwd_send, con_recv, ids_send, ids_recv, par_send, par_recv, mov_send, mov_recv,
):
    inner = rows // OUTER
    local = bands * slots
    per_chunk = local // CHUNKS
    row = lax.axis_index("row")
    col = lax.axis_index("col")
    outer_at = row // inner
    inner_at = lax.rem(row, inner)

    def place(dz, dy):
        return lax.rem(outer_at + dz + OUTER, OUTER) * inner + lax.rem(inner_at + dy + inner, inner)

    tile_copies = [
        pltpu.make_async_copy(tiles_hbm.at[b], tiles.at[b], tile_sem.at[b]) for b in range(bands)
    ]
    for copy in tile_copies:
        copy.start()
    in_copies = [
        pltpu.make_async_copy(src, dst, in_sem.at[i])
        for i, (src, dst) in enumerate(
            [(primal_hbm, primal), (cost_hbm, cost), (lower_hbm, lower), (upper_hbm, upper), (kinds_hbm, kinds)]
        )
    ]
    for copy in in_copies:
        copy.start()

    barrier = pltpu.get_barrier_semaphore()
    for d in range(1, rows):
        pl.semaphore_signal(barrier, 1, device_id={"row": lax.rem(row + d, rows)}, device_id_type=MESH_ID)
    for d in range(1, cols):
        pl.semaphore_signal(barrier, 1, device_id={"col": lax.rem(col + d, cols)}, device_id_type=MESH_ID)

    pending = []

    def remote(src, dst, send, recv, target):
        copy = pltpu.make_async_remote_copy(
            src_ref=src, dst_ref=dst, send_sem=send, recv_sem=recv,
            device_id=target, device_id_type=MESH_ID,
        )
        copy.start()
        pending.append(copy)

    def await_recv(ref, recv):
        pltpu.make_async_copy(ref, ref, recv).wait()

    lane_block = lax.broadcasted_iota(jnp.int32, (GROUP, GROUP * width), 1) // width
    row_at = lax.broadcasted_iota(jnp.int32, (GROUP, GROUP * width), 0)
    diagonal = lane_block == row_at

    def transposed(it, source, first, count):
        def band(b, carry):
            line = source[pl.ds(b, 1), :]
            wide = jnp.concatenate([jnp.broadcast_to(line, (GROUP, width))] * GROUP, axis=1)
            left = jnp.where(diagonal, wide, 0.0).astype(jnp.bfloat16)
            for g in range(slots // GROUP):
                right = tiles[b, g * GROUP:(g + 1) * GROUP].reshape(GROUP * width, width)
                value = jnp.dot(left, right, preferred_element_type=jnp.float32)
                at = pl.multiple_of(b * slots + g * GROUP, GROUP)
                high = value.astype(jnp.bfloat16)
                low = (value - high.astype(jnp.float32)).astype(jnp.bfloat16)
                contrib[it, row, pl.ds(at, GROUP), :width] = high
                contrib[it, row, pl.ds(at, GROUP), width:] = low
            return carry

        lax.fori_loop(first, first + count, band, 0, unroll=True)

    def chunk_ref(it, src, c):
        return contrib.at[it, src, pl.ds(c * per_chunk, per_chunk), :]

    def send_chunk(it, c):
        for dy in range(1, inner):
            remote(chunk_ref(it, row, c), chunk_ref(it, row, c), own_send.at[it, 0, dy, c],
                   con_recv.at[it, 0, dy, c], {"row": place(0, dy)})
        for dz in range(1, OUTER):
            remote(chunk_ref(it, row, c), chunk_ref(it, row, c), own_send.at[it, dz, 0, c],
                   con_recv.at[it, dz, 0, c], {"row": place(dz, 0)})

    def forward_chunks(it, meanwhile):
        for dz in range(1, OUTER):
            src = place(-dz, 0)
            for c in range(CHUNKS):
                await_recv(chunk_ref(it, src, c), con_recv.at[it, dz, 0, c])
                for dy in range(1, inner):
                    remote(chunk_ref(it, src, c), chunk_ref(it, src, c), fwd_send.at[it, dz, dy, c],
                           con_recv.at[it, dz, dy, c], {"row": place(0, dy)})
            meanwhile(dz)

    def gather_rest(it):
        for dz in range(OUTER):
            for dy in range(1, inner):
                for c in range(CHUNKS):
                    await_recv(chunk_ref(it, place(-dz, -dy), c), con_recv.at[it, dz, dy, c])

    def build_hot(src):
        line = ids_all[pl.ds(src, 1), 0, :]

        def part(i, carry):
            at = pl.multiple_of(i * 128, 128)
            index = lax.broadcasted_iota(jnp.int32, (128, local), 0) + at
            hot[src, pl.ds(at, 128), :] = jnp.where(index == line, 1.0, 0.0).astype(jnp.bfloat16)
            return carry

        lax.fori_loop(0, blocks // 128, part, 0)

    def primal_update(it, primal_step):
        size = 128

        def part(i, moved):
            at = pl.multiple_of(i * size, size)
            here = pl.ds(at, size)
            product = jnp.zeros((size, 2 * width), jnp.float32)
            for src in range(rows):
                product = product + jnp.dot(hot[src, here, :], contrib[it, src], preferred_element_type=jnp.float32)
            product = product[:, :width] + product[:, width:]
            old = primal[here, :] if it == 0 else result[here, :]
            new = project_primal(
                old - primal_step * (cost[here, :] - product), lower[here, :], upper[here, :], kinds[here, :]
            )
            result[here, :] = new
            xbar[here, :] = (2.0 * new - old).astype(jnp.bfloat16)
            square = (new - old) ** 2
            return moved + jnp.sum(square.reshape(size // 8, 8, width), axis=0)

        return lax.fori_loop(0, blocks // size, part, jnp.zeros((8, width), jnp.float32), unroll=2)

    def forward(it):
        picked[...] = jnp.dot(hot_own[...], xbar[...], preferred_element_type=jnp.float32).astype(jnp.bfloat16)

        def band(b, carry):
            total = jnp.zeros((GROUP, GROUP * width), jnp.float32)
            for g in range(slots // GROUP):
                right = tiles[b, g * GROUP:(g + 1) * GROUP].reshape(GROUP * width, width)
                at = pl.multiple_of(b * slots + g * GROUP, GROUP)
                total = total + lax.dot_general(
                    picked[pl.ds(at, GROUP), :], right, (((1,), (1,)), ((), ())),
                    preferred_element_type=jnp.float32,
                )
            total = jnp.where(diagonal, total, 0.0)
            lanes = total[:, :width]
            for k in range(1, GROUP):
                lanes = lanes + total[:, k * width:(k + 1) * width]
            partial[it, col, pl.ds(b, 1), :] = jnp.sum(lanes, axis=0, keepdims=True)
            return carry

        lax.fori_loop(0, bands, band, 0, unroll=True)

    def exchange_partials(it):
        for d in range(1, cols):
            remote(partial.at[it, col], partial.at[it, col], par_send.at[it, d], par_recv.at[it, d],
                   {"col": lax.rem(col + d, cols)})
        for d in range(1, cols):
            await_recv(partial.at[it, lax.rem(col + cols - d, cols)], par_recv.at[it, d])
        total = partial[it, 0]
        for c in range(1, cols):
            total = total + partial[it, c]
        return total

    ids_all[row] = ids_row[...]

    per_bands = bands // CHUNKS
    for c in range(CHUNKS):
        for b in range(c * per_bands, (c + 1) * per_bands):
            tile_copies[b].wait()
        transposed(0, dual_ref, c * per_bands, per_bands)
        if c == 0:
            pl.semaphore_wait(barrier, rows + cols - 2)
        send_chunk(0, c)
    for d in range(1, rows):
        remote(ids_all.at[row], ids_all.at[row], ids_send.at[d], ids_recv.at[d], {"row": lax.rem(row + d, rows)})
    index = lax.broadcasted_iota(jnp.int32, (local, blocks), 1)
    hot_own[...] = jnp.where(index == ids_col[...], 1.0, 0.0).astype(jnp.bfloat16)
    build_hot(row)
    for copy in in_copies:
        copy.wait()
    for d in range(1, rows):
        await_recv(ids_all.at[lax.rem(row + rows - d, rows)], ids_recv.at[d])

    def build_hots(dz):
        for dy in range(inner):
            build_hot(place(-dz, -dy))

    forward_chunks(0, build_hots)
    for dy in range(1, inner):
        build_hot(place(0, -dy))
    gather_rest(0)
    moved_primal = primal_update(0, step_size)
    partial[0, col, 8:16, :] = moved_primal
    forward(0)
    total = exchange_partials(0)
    dual = dual_ref[...]
    dual_one = project_dual(dual + step_size * (right_ref[...] - total[:bands]), row_kinds_ref[...])
    dual_out[...] = dual_one
    moved_dual[row] = (dual_one - dual) ** 2
    moved_primal = jnp.sum(total[8:16], keepdims=True)

    for d in range(1, rows):
        remote(moved_dual.at[row], moved_dual.at[row], mov_send.at[d], mov_recv.at[d],
               {"row": lax.rem(row + d, rows)})
    for c in range(CHUNKS):
        transposed(1, dual_out, c * per_bands, per_bands)
        send_chunk(1, c)
    for d in range(1, rows):
        await_recv(moved_dual.at[lax.rem(row + rows - d, rows)], mov_recv.at[d])
    squares = moved_dual[0]
    for r in range(1, rows):
        squares = squares + moved_dual[r]
    weight = jnp.sqrt(jnp.sqrt((jnp.sum(squares, keepdims=True) + epsilon) / (moved_primal + epsilon)))
    forward_chunks(1, lambda dz: None)
    gather_rest(1)
    primal_update(1, step_size / weight)
    out_copy = pltpu.make_async_copy(result, primal_out, out_sem)
    out_copy.start()
    partial[1, col, 8:16, :] = jnp.zeros((8, width), jnp.float32)
    forward(1)
    total = exchange_partials(1)
    dual_out[...] = project_dual(
        dual_one + (step_size * weight) * (right_ref[...] - total[:bands]), row_kinds_ref[...]
    )
    for copy in pending:
        copy.wait_send()
    out_copy.wait()


def per_device(
    rows, cols,
    tile_values, block_cols, primal_start, dual_start, cost_vector,
    lower_bound, upper_bound, var_kinds, right_side, row_kinds,
):
    bands, slots, width, _ = tile_values.shape
    blocks = primal_start.shape[0] // width
    local = bands * slots
    inner = rows // OUTER
    ids = block_cols - lax.axis_index("col") * blocks
    vmem = pl.BlockSpec(memory_space=pltpu.VMEM)
    hbm = pl.BlockSpec(memory_space=pl.ANY)
    dma = pltpu.SemaphoreType.DMA
    tall = (blocks, width)
    primal_final, dual_final = pl.pallas_call(
        functools.partial(kernel, rows, cols, bands, slots, width, blocks),
        out_shape=(
            jax.ShapeDtypeStruct(tall, jnp.float32),
            jax.ShapeDtypeStruct((bands, width), jnp.float32),
        ),
        in_specs=[hbm, vmem, vmem] + [hbm] * 5 + [vmem] * 3,
        out_specs=(hbm, vmem),
        scratch_shapes=[
            pltpu.VMEM((bands, slots, width, width), jnp.bfloat16),
            pltpu.VMEM(tall, jnp.float32),
            pltpu.VMEM(tall, jnp.float32),
            pltpu.VMEM(tall, jnp.float32),
            pltpu.VMEM(tall, jnp.float32),
            pltpu.VMEM(tall, jnp.int32),
            pltpu.VMEM(tall, jnp.float32),
            pltpu.VMEM((rows, blocks, local), jnp.bfloat16),
            pltpu.VMEM((local, blocks), jnp.bfloat16),
            pltpu.VMEM(tall, jnp.bfloat16),
            pltpu.VMEM((local, width), jnp.bfloat16),
            pltpu.VMEM((2, rows, local, 2 * width), jnp.bfloat16),
            pltpu.VMEM((rows, 1, local), jnp.int32),
            pltpu.VMEM((2, cols, 16, width), jnp.float32),
            pltpu.VMEM((rows, bands, width), jnp.float32),
            dma((bands,)),
            dma((5,)),
            dma,
            dma((2, OUTER, inner, CHUNKS)),
            dma((2, OUTER, inner, CHUNKS)),
            dma((2, OUTER, inner, CHUNKS)),
            dma((rows,)),
            dma((rows,)),
            dma((2, cols)),
            dma((2, cols)),
            dma((rows,)),
            dma((rows,)),
        ],
        compiler_params=pltpu.CompilerParams(
            collective_id=0, has_side_effects=True, vmem_limit_bytes=56 * 1024 * 1024
        ),
    )(
        tile_values,
        ids.reshape(1, local),
        ids.reshape(local, 1),
        primal_start.reshape(tall),
        cost_vector.reshape(tall),
        lower_bound.reshape(tall),
        upper_bound.reshape(tall),
        var_kinds.reshape(tall),
        dual_start.reshape(bands, width),
        right_side.reshape(bands, width),
        row_kinds.reshape(bands, width),
    )
    return primal_final.reshape(-1), dual_final.reshape(-1)


def solution(mesh):
    return jax.shard_map(
        functools.partial(per_device, mesh.shape["row"], mesh.shape["col"]),
        mesh=mesh,
        in_specs=(
            P("row", "col", None, None),
            P("row", "col"),
            P("col"),
            P("row"),
            P("col"),
            P("col"),
            P("col"),
            P("col"),
            P("row"),
            P("row"),
        ),
        out_specs=(P("col"), P("row")),
        check_vma=False,
    )
```

```python
import functools

import jax
import jax.numpy as jnp
from jax import lax
from jax.experimental import pallas as pl
from jax.experimental.pallas import tpu as pltpu
from jax.sharding import PartitionSpec as P

step_size = 0.8
epsilon = 1e-06
OUTER = 4
GROUP = 16
CHUNKS = 2
MESH_ID = pl.DeviceIdType.MESH


def project_primal(vector, lower_bound, upper_bound, var_kinds):
    raised = jnp.where(var_kinds >= 1, jnp.maximum(vector, lower_bound), vector)
    return jnp.where(var_kinds == 2, jnp.minimum(raised, upper_bound), raised)


def project_dual(vector, row_kinds):
    return jnp.where(row_kinds == 1, jnp.maximum(vector, 0.0), vector)


def kernel(
    rows, cols, bands, slots, width, blocks,
    tiles_hbm, ids_row, ids_col, primal_hbm, cost_hbm, lower_hbm, upper_hbm, kinds_hbm,
    dual_ref, right_ref, row_kinds_ref,
    primal_out, dual_out,
    tiles, primal, cost, lower, upper, kinds, mine, result,
    hot, hot_own, spread, picked, contrib, ids_all, stage, arrived, partial, moved,
    tile_sem, in_sem, out_sem,
    con_send, con_recv, sum_send, sum_recv, own_send, fwd_send, spr_recv, ids_send, ids_recv, par_send, par_recv, mov_send, mov_recv,
):
    inner = rows // OUTER
    local = bands * slots
    per_chunk = local // CHUNKS
    row = lax.axis_index("row")
    col = lax.axis_index("col")
    outer_at = row // inner
    inner_at = lax.rem(row, inner)
    part_rows = blocks // inner
    own_rows = blocks // rows

    def owned(outer_place, inner_place):
        return pl.ds(pl.multiple_of(inner_place * part_rows + outer_place * own_rows, own_rows), own_rows)

    own = owned(outer_at, inner_at)

    def place(dz, dy):
        return lax.rem(outer_at + dz + OUTER, OUTER) * inner + lax.rem(inner_at + dy + inner, inner)

    tile_copies = [
        pltpu.make_async_copy(tiles_hbm.at[b], tiles.at[b], tile_sem.at[b]) for b in range(bands)
    ]
    for copy in tile_copies:
        copy.start()
    in_copies = [
        pltpu.make_async_copy(src.at[own, :], dst, in_sem.at[i])
        for i, (src, dst) in enumerate(
            [(primal_hbm, primal), (cost_hbm, cost), (lower_hbm, lower), (upper_hbm, upper), (kinds_hbm, kinds)]
        )
    ]
    for copy in in_copies:
        copy.start()

    barrier = pltpu.get_barrier_semaphore()
    for d in range(1, rows):
        pl.semaphore_signal(barrier, 1, device_id={"row": lax.rem(row + d, rows)}, device_id_type=MESH_ID)
    for d in range(1, cols):
        pl.semaphore_signal(barrier, 1, device_id={"col": lax.rem(col + d, cols)}, device_id_type=MESH_ID)

    pending = []

    def remote(src, dst, send, recv, target):
        copy = pltpu.make_async_remote_copy(
            src_ref=src, dst_ref=dst, send_sem=send, recv_sem=recv,
            device_id=target, device_id_type=MESH_ID,
        )
        copy.start()
        pending.append(copy)

    def await_recv(ref, recv):
        pltpu.make_async_copy(ref, ref, recv).wait()

    lane_block = lax.broadcasted_iota(jnp.int32, (GROUP, GROUP * width), 1) // width
    row_at = lax.broadcasted_iota(jnp.int32, (GROUP, GROUP * width), 0)
    diagonal = lane_block == row_at

    def transposed(it, source, first, count):
        def band(b, carry):
            line = source[pl.ds(b, 1), :]
            wide = jnp.concatenate([jnp.broadcast_to(line, (GROUP, width))] * GROUP, axis=1)
            left = jnp.where(diagonal, wide, 0.0).astype(jnp.bfloat16)
            for g in range(slots // GROUP):
                right = tiles[b, g * GROUP:(g + 1) * GROUP].reshape(GROUP * width, width)
                value = jnp.dot(left, right, preferred_element_type=jnp.float32)
                at = pl.multiple_of(b * slots + g * GROUP, GROUP)
                high = value.astype(jnp.bfloat16)
                low = (value - high.astype(jnp.float32)).astype(jnp.bfloat16)
                contrib[it, inner_at, pl.ds(at, GROUP), :width] = high
                contrib[it, inner_at, pl.ds(at, GROUP), width:] = low
            return carry

        lax.fori_loop(first, first + count, band, 0, unroll=True)

    def chunk_ref(it, src, c):
        return contrib.at[it, src, pl.ds(c * per_chunk, per_chunk), :]

    def send_chunk(it, c):
        for dy in range(1, inner):
            remote(chunk_ref(it, inner_at, c), chunk_ref(it, inner_at, c), con_send.at[it, dy, c],
                   con_recv.at[it, dy, c], {"row": place(0, dy)})

    def spread_start(k):
        for dz in range(1, OUTER):
            remote(spread.at[k, own, :], spread.at[k, own, :], own_send.at[k, dz, 0],
                   spr_recv.at[k, dz, 0], {"row": place(dz, 0)})
        for dy in range(1, inner):
            remote(spread.at[k, own, :], spread.at[k, own, :], own_send.at[k, 0, dy],
                   spr_recv.at[k, 0, dy], {"row": place(0, dy)})

    def spread_finish(k):
        for dz in range(1, OUTER):
            here = spread.at[k, owned(lax.rem(outer_at + OUTER - dz, OUTER), inner_at), :]
            await_recv(here, spr_recv.at[k, dz, 0])
            for dy in range(1, inner):
                remote(here, here, fwd_send.at[k, dz, dy], spr_recv.at[k, dz, dy], {"row": place(0, dy)})
        for dz in range(OUTER):
            for dy in range(1, inner):
                there = owned(lax.rem(outer_at + OUTER - dz, OUTER), lax.rem(inner_at + inner - dy, inner))
                await_recv(spread.at[k, there, :], spr_recv.at[k, dz, dy])

    def build_hot(src):
        line = ids_all[src] - inner_at * part_rows

        def part(i, carry):
            at = pl.multiple_of(i * 64, 64)
            index = lax.broadcasted_iota(jnp.int32, (64, local), 0) + at
            hot[src, pl.ds(at, 64), :] = jnp.where(index == line, 1.0, 0.0).astype(jnp.bfloat16)
            return carry

        lax.fori_loop(0, part_rows // 64, part, 0)

    def reduce_to_owner(it):
        for dy in range(1, inner):
            for c in range(CHUNKS):
                await_recv(chunk_ref(it, lax.rem(inner_at + inner - dy, inner), c), con_recv.at[it, dy, c])
        for dz in list(range(1, OUTER)) + [0]:
            target = lax.rem(outer_at + dz, OUTER)
            at = pl.ds(pl.multiple_of(target * own_rows, own_rows), own_rows)
            product = jnp.zeros((own_rows, 2 * width), jnp.float32)
            for src in range(inner):
                product = product + jnp.dot(hot[src, at, :], contrib[it, src], preferred_element_type=jnp.float32)
            product = product[:, :width] + product[:, width:]
            if dz == 0:
                arrived[it, outer_at] = product
            else:
                stage[it, dz] = product
                remote(stage.at[it, dz], arrived.at[it, outer_at], sum_send.at[it, dz], sum_recv.at[it, dz],
                       {"row": place(dz, 0)})
        for dz in range(1, OUTER):
            await_recv(arrived.at[it, lax.rem(outer_at + OUTER - dz, OUTER)], sum_recv.at[it, dz])
        total = arrived[it, 0]
        for z in range(1, OUTER):
            total = total + arrived[it, z]
        return total

    def primal_update(it, primal_step):
        product = reduce_to_owner(it)
        old = primal[...] if it == 0 else mine[...]
        new = project_primal(old - primal_step * (cost[...] - product), lower[...], upper[...], kinds[...])
        spread[it, own, :] = (2.0 * new - old).astype(jnp.bfloat16)
        spread_start(it)
        if it == 0:
            mine[...] = new
        else:
            spread[2, own, :] = new.astype(jnp.bfloat16)
            spread_start(2)
        return jnp.sum(((new - old) ** 2).reshape(own_rows // 8, 8, width), axis=0)

    def forward(it):
        picked[...] = jnp.dot(hot_own[...], spread[it], preferred_element_type=jnp.float32).astype(jnp.bfloat16)

        def band(b, carry):
            total = jnp.zeros((GROUP, GROUP * width), jnp.float32)
            for g in range(slots // GROUP):
                right = tiles[b, g * GROUP:(g + 1) * GROUP].reshape(GROUP * width, width)
                at = pl.multiple_of(b * slots + g * GROUP, GROUP)
                total = total + lax.dot_general(
                    picked[pl.ds(at, GROUP), :], right, (((1,), (1,)), ((), ())),
                    preferred_element_type=jnp.float32,
                )
            total = jnp.where(diagonal, total, 0.0)
            lanes = total[:, :width]
            for k in range(1, GROUP):
                lanes = lanes + total[:, k * width:(k + 1) * width]
            partial[it, col, pl.ds(b, 1), :] = jnp.sum(lanes, axis=0, keepdims=True)
            return carry

        lax.fori_loop(0, bands, band, 0, unroll=True)

    def send_partials(it):
        for d in range(1, cols):
            remote(partial.at[it, col], partial.at[it, col], par_send.at[it, d], par_recv.at[it, d],
                   {"col": lax.rem(col + d, cols)})

    def sum_partials(it):
        for d in range(1, cols):
            await_recv(partial.at[it, lax.rem(col + cols - d, cols)], par_recv.at[it, d])
        total = partial[it, 0]
        for c in range(1, cols):
            total = total + partial[it, c]
        return total

    ids_all[inner_at] = ids_row[...]

    pl.semaphore_wait(barrier, rows + cols - 2)
    for d in range(1, inner):
        remote(ids_all.at[inner_at], ids_all.at[inner_at], ids_send.at[d], ids_recv.at[d], {"row": place(0, d)})
    per_bands = bands // CHUNKS
    for c in range(CHUNKS):
        for b in range(c * per_bands, (c + 1) * per_bands):
            tile_copies[b].wait()
        transposed(0, dual_ref, c * per_bands, per_bands)
        send_chunk(0, c)
    for d in range(1, inner):
        await_recv(ids_all.at[lax.rem(inner_at + inner - d, inner)], ids_recv.at[d])
    for src in range(inner):
        build_hot(src)
    index = lax.broadcasted_iota(jnp.int32, (local, blocks), 1)
    hot_own[...] = jnp.where(index == ids_col[...], 1.0, 0.0).astype(jnp.bfloat16)
    for copy in in_copies:
        copy.wait()
    partial[0, col, 8:16, :] = primal_update(0, step_size)
    spread_finish(0)
    forward(0)
    send_partials(0)
    total = sum_partials(0)
    dual = dual_ref[...]
    dual_one = project_dual(dual + step_size * (right_ref[...] - total[:bands]), row_kinds_ref[...])
    dual_out[...] = dual_one
    moved[row, :bands, :] = (dual_one - dual) ** 2
    moved[row, bands:, :] = total[8:16]

    for c in range(CHUNKS):
        transposed(1, dual_out, c * per_bands, per_bands)
        send_chunk(1, c)
        if c == 0:
            for d in range(1, rows):
                remote(moved.at[row], moved.at[row], mov_send.at[d], mov_recv.at[d],
                       {"row": lax.rem(row + d, rows)})
    for d in range(1, rows):
        await_recv(moved.at[lax.rem(row + rows - d, rows)], mov_recv.at[d])
    squares = moved[0]
    for r in range(1, rows):
        squares = squares + moved[r]
    dual_moved = jnp.sum(squares[:bands], keepdims=True)
    primal_moved = jnp.sum(squares[bands:], keepdims=True)
    weight = jnp.sqrt(jnp.sqrt((dual_moved + epsilon) / (primal_moved + epsilon)))
    primal_update(1, step_size / weight)
    partial[1, col, 8:16, :] = jnp.zeros((8, width), jnp.float32)
    spread_finish(1)
    forward(1)
    send_partials(1)
    spread_finish(2)
    result[...] = spread[2].astype(jnp.float32)
    out_copy = pltpu.make_async_copy(result, primal_out, out_sem)
    out_copy.start()
    total = sum_partials(1)
    dual_out[...] = project_dual(
        dual_one + (step_size * weight) * (right_ref[...] - total[:bands]), row_kinds_ref[...]
    )
    for copy in pending:
        copy.wait_send()
    out_copy.wait()


def per_device(
    rows, cols,
    tile_values, block_cols, primal_start, dual_start, cost_vector,
    lower_bound, upper_bound, var_kinds, right_side, row_kinds,
):
    bands, slots, width, _ = tile_values.shape
    blocks = primal_start.shape[0] // width
    local = bands * slots
    inner = rows // OUTER
    ids = block_cols - lax.axis_index("col") * blocks
    vmem = pl.BlockSpec(memory_space=pltpu.VMEM)
    hbm = pl.BlockSpec(memory_space=pl.ANY)
    dma = pltpu.SemaphoreType.DMA
    tall = (blocks, width)
    short = (blocks // rows, width)
    primal_final, dual_final = pl.pallas_call(
        functools.partial(kernel, rows, cols, bands, slots, width, blocks),
        out_shape=(
            jax.ShapeDtypeStruct(tall, jnp.float32),
            jax.ShapeDtypeStruct((bands, width), jnp.float32),
        ),
        in_specs=[hbm, vmem, vmem] + [hbm] * 5 + [vmem] * 3,
        out_specs=(hbm, vmem),
        scratch_shapes=[
            pltpu.VMEM((bands, slots, width, width), jnp.bfloat16),
            pltpu.VMEM(short, jnp.float32),
            pltpu.VMEM(short, jnp.float32),
            pltpu.VMEM(short, jnp.float32),
            pltpu.VMEM(short, jnp.float32),
            pltpu.VMEM(short, jnp.int32),
            pltpu.VMEM(short, jnp.float32),
            pltpu.VMEM(tall, jnp.float32),
            pltpu.VMEM((inner, blocks // inner, local), jnp.bfloat16),
            pltpu.VMEM((local, blocks), jnp.bfloat16),
            pltpu.VMEM((3,) + tall, jnp.bfloat16),
            pltpu.VMEM((local, width), jnp.bfloat16),
            pltpu.VMEM((2, inner, local, 2 * width), jnp.bfloat16),
            pltpu.VMEM((inner, 1, local), jnp.int32),
            pltpu.VMEM((2, OUTER) + short, jnp.float32),
            pltpu.VMEM((2, OUTER) + short, jnp.float32),
            pltpu.VMEM((2, cols, 16, width), jnp.float32),
            pltpu.VMEM((rows, bands + 8, width), jnp.float32),
            dma((bands,)),
            dma((5,)),
            dma,
            dma((2, inner, CHUNKS)),
            dma((2, inner, CHUNKS)),
            dma((2, OUTER)),
            dma((2, OUTER)),
            dma((3, OUTER, inner)),
            dma((3, OUTER, inner)),
            dma((3, OUTER, inner)),
            dma((inner,)),
            dma((inner,)),
            dma((2, cols)),
            dma((2, cols)),
            dma((rows,)),
            dma((rows,)),
        ],
        compiler_params=pltpu.CompilerParams(
            collective_id=0, has_side_effects=True, vmem_limit_bytes=56 * 1024 * 1024
        ),
    )(
        tile_values,
        ids.reshape(1, local),
        ids.reshape(local, 1),
        primal_start.reshape(tall),
        cost_vector.reshape(tall),
        lower_bound.reshape(tall),
        upper_bound.reshape(tall),
        var_kinds.reshape(tall),
        dual_start.reshape(bands, width),
        right_side.reshape(bands, width),
        row_kinds.reshape(bands, width),
    )
    return primal_final.reshape(-1), dual_final.reshape(-1)


def solution(mesh):
    return jax.shard_map(
        functools.partial(per_device, mesh.shape["row"], mesh.shape["col"]),
        mesh=mesh,
        in_specs=(
            P("row", "col", None, None),
            P("row", "col"),
            P("col"),
            P("row"),
            P("col"),
            P("col"),
            P("col"),
            P("col"),
            P("row"),
            P("row"),
        ),
        out_specs=(P("col"), P("row")),
        check_vma=False,
    )
```

```python
import functools

import jax
import jax.numpy as jnp
from jax import lax
from jax.experimental import pallas as pl
from jax.experimental.pallas import tpu as pltpu
from jax.sharding import PartitionSpec as P

step_size = 0.8
epsilon = 1e-06
OUTER = 4
GROUP = 16
CHUNKS = 2
MESH_ID = pl.DeviceIdType.MESH


def project_primal(vector, lower_bound, upper_bound, var_kinds):
    raised = jnp.where(var_kinds >= 1, jnp.maximum(vector, lower_bound), vector)
    return jnp.where(var_kinds == 2, jnp.minimum(raised, upper_bound), raised)


def project_dual(vector, row_kinds):
    return jnp.where(row_kinds == 1, jnp.maximum(vector, 0.0), vector)


def kernel(
    rows, cols, bands, slots, width, blocks,
    tiles_hbm, ids_row, ids_col, primal_hbm, cost_hbm, lower_hbm, upper_hbm, kinds_hbm,
    dual_ref, right_ref, row_kinds_ref,
    primal_out, dual_out,
    tiles, primal, cost, lower, upper, kinds, mine, result,
    hot, hot_own, spread, picked, contrib, ids_all, stage, arrived, partial, moved,
    tile_sem, in_sem, out_sem,
    con_send, con_recv, sum_send, sum_recv, own_send, fwd_send, spr_recv, ids_send, ids_recv, par_send, par_recv, mov_send, mov_recv,
):
    inner = rows // OUTER
    local = bands * slots
    per_chunk = local // CHUNKS
    row = lax.axis_index("row")
    col = lax.axis_index("col")
    outer_at = row // inner
    inner_at = lax.rem(row, inner)
    part_rows = blocks // inner
    own_rows = blocks // rows

    def owned(outer_place, inner_place):
        return pl.ds(pl.multiple_of(inner_place * part_rows + outer_place * own_rows, own_rows), own_rows)

    own = owned(outer_at, inner_at)

    def place(dz, dy):
        return lax.rem(outer_at + dz + OUTER, OUTER) * inner + lax.rem(inner_at + dy + inner, inner)

    tile_copies = [
        pltpu.make_async_copy(tiles_hbm.at[b], tiles.at[b], tile_sem.at[b]) for b in range(bands)
    ]
    for copy in tile_copies:
        copy.start()
    in_copies = [
        pltpu.make_async_copy(src.at[own, :], dst, in_sem.at[i])
        for i, (src, dst) in enumerate(
            [(primal_hbm, primal), (cost_hbm, cost), (lower_hbm, lower), (upper_hbm, upper), (kinds_hbm, kinds)]
        )
    ]
    for copy in in_copies:
        copy.start()

    barrier = pltpu.get_barrier_semaphore()
    for d in range(1, rows):
        pl.semaphore_signal(barrier, 1, device_id={"row": lax.rem(row + d, rows)}, device_id_type=MESH_ID)
    for d in range(1, cols):
        pl.semaphore_signal(barrier, 1, device_id={"col": lax.rem(col + d, cols)}, device_id_type=MESH_ID)

    pending = []

    def remote(src, dst, send, recv, target):
        copy = pltpu.make_async_remote_copy(
            src_ref=src, dst_ref=dst, send_sem=send, recv_sem=recv,
            device_id=target, device_id_type=MESH_ID,
        )
        copy.start()
        pending.append(copy)

    def await_recv(ref, recv):
        pltpu.make_async_copy(ref, ref, recv).wait()

    lane_block = lax.broadcasted_iota(jnp.int32, (GROUP, GROUP * width), 1) // width
    row_at = lax.broadcasted_iota(jnp.int32, (GROUP, GROUP * width), 0)
    diagonal = lane_block == row_at

    def transposed(it, source, first, count):
        def band(b, carry):
            line = source[pl.ds(b, 1), :]
            wide = jnp.concatenate([jnp.broadcast_to(line, (GROUP, width))] * GROUP, axis=1)
            left = jnp.where(diagonal, wide, 0.0).astype(jnp.bfloat16)
            for g in range(slots // GROUP):
                right = tiles[b, g * GROUP:(g + 1) * GROUP].reshape(GROUP * width, width)
                value = jnp.dot(left, right, preferred_element_type=jnp.float32)
                at = pl.multiple_of(b * slots + g * GROUP, GROUP)
                high = value.astype(jnp.bfloat16)
                low = (value - high.astype(jnp.float32)).astype(jnp.bfloat16)
                contrib[it, inner_at, pl.ds(at, GROUP), :width] = high
                contrib[it, inner_at, pl.ds(at, GROUP), width:] = low
            return carry

        lax.fori_loop(first, first + count, band, 0, unroll=True)

    def chunk_ref(it, src, c):
        return contrib.at[it, src, pl.ds(c * per_chunk, per_chunk), :]

    def send_chunk(it, c):
        for dy in range(1, inner):
            remote(chunk_ref(it, inner_at, c), chunk_ref(it, inner_at, c), con_send.at[it, dy, c],
                   con_recv.at[it, dy, c], {"row": place(0, dy)})

    def spread_ref(k, at):
        return result.at[at, :] if k == 2 else spread.at[k, at, :]

    def spread_start(k):
        for dz in range(1, OUTER):
            remote(spread_ref(k, own), spread_ref(k, own), own_send.at[k, dz, 0],
                   spr_recv.at[k, dz, 0], {"row": place(dz, 0)})
        for dy in range(1, inner):
            remote(spread_ref(k, own), spread_ref(k, own), own_send.at[k, 0, dy],
                   spr_recv.at[k, 0, dy], {"row": place(0, dy)})

    def spread_finish(k):
        for dz in range(1, OUTER):
            here = spread_ref(k, owned(lax.rem(outer_at + OUTER - dz, OUTER), inner_at))
            await_recv(here, spr_recv.at[k, dz, 0])
            for dy in range(1, inner):
                remote(here, here, fwd_send.at[k, dz, dy], spr_recv.at[k, dz, dy], {"row": place(0, dy)})
        for dz in range(OUTER):
            for dy in range(1, inner):
                there = owned(lax.rem(outer_at + OUTER - dz, OUTER), lax.rem(inner_at + inner - dy, inner))
                await_recv(spread_ref(k, there), spr_recv.at[k, dz, dy])

    def build_hot(src):
        line = ids_all[src] - inner_at * part_rows

        def part(i, carry):
            at = pl.multiple_of(i * 64, 64)
            index = lax.broadcasted_iota(jnp.int32, (64, local), 0) + at
            hot[src, pl.ds(at, 64), :] = jnp.where(index == line, 1.0, 0.0).astype(jnp.bfloat16)
            return carry

        lax.fori_loop(0, part_rows // 64, part, 0)

    def reduce_to_owner(it):
        for dy in range(1, inner):
            for c in range(CHUNKS):
                await_recv(chunk_ref(it, lax.rem(inner_at + inner - dy, inner), c), con_recv.at[it, dy, c])
        for dz in list(range(1, OUTER)) + [0]:
            target = lax.rem(outer_at + dz, OUTER)
            at = pl.ds(pl.multiple_of(target * own_rows, own_rows), own_rows)
            product = jnp.zeros((own_rows, 2 * width), jnp.float32)
            for src in range(inner):
                product = product + jnp.dot(hot[src, at, :], contrib[it, src], preferred_element_type=jnp.float32)
            product = product[:, :width] + product[:, width:]
            if dz == 0:
                arrived[it, outer_at] = product
            else:
                stage[it, dz] = product
                remote(stage.at[it, dz], arrived.at[it, outer_at], sum_send.at[it, dz], sum_recv.at[it, dz],
                       {"row": place(dz, 0)})
        for dz in range(1, OUTER):
            await_recv(arrived.at[it, lax.rem(outer_at + OUTER - dz, OUTER)], sum_recv.at[it, dz])
        total = arrived[it, 0]
        for z in range(1, OUTER):
            total = total + arrived[it, z]
        return total

    def primal_update(it, primal_step):
        product = reduce_to_owner(it)
        old = primal[...] if it == 0 else mine[...]
        new = project_primal(old - primal_step * (cost[...] - product), lower[...], upper[...], kinds[...])
        spread[it, own, :] = (2.0 * new - old).astype(jnp.bfloat16)
        spread_start(it)
        if it == 0:
            mine[...] = new
        else:
            result[own, :] = new
            spread_start(2)
        return jnp.sum(((new - old) ** 2).reshape(own_rows // 8, 8, width), axis=0)

    def forward(it):
        picked[...] = jnp.dot(hot_own[...], spread[it], preferred_element_type=jnp.float32).astype(jnp.bfloat16)

        def band(b, carry):
            total = jnp.zeros((GROUP, GROUP * width), jnp.float32)
            for g in range(slots // GROUP):
                right = tiles[b, g * GROUP:(g + 1) * GROUP].reshape(GROUP * width, width)
                at = pl.multiple_of(b * slots + g * GROUP, GROUP)
                total = total + lax.dot_general(
                    picked[pl.ds(at, GROUP), :], right, (((1,), (1,)), ((), ())),
                    preferred_element_type=jnp.float32,
                )
            total = jnp.where(diagonal, total, 0.0)
            lanes = total[:, :width]
            for k in range(1, GROUP):
                lanes = lanes + total[:, k * width:(k + 1) * width]
            partial[it, col, pl.ds(b, 1), :] = jnp.sum(lanes, axis=0, keepdims=True)
            return carry

        lax.fori_loop(0, bands, band, 0, unroll=True)

    def send_partials(it):
        for d in range(1, cols):
            remote(partial.at[it, col], partial.at[it, col], par_send.at[it, d], par_recv.at[it, d],
                   {"col": lax.rem(col + d, cols)})

    def sum_partials(it):
        for d in range(1, cols):
            await_recv(partial.at[it, lax.rem(col + cols - d, cols)], par_recv.at[it, d])
        total = partial[it, 0]
        for c in range(1, cols):
            total = total + partial[it, c]
        return total

    ids_all[inner_at] = ids_row[...]

    pl.semaphore_wait(barrier, rows + cols - 2)
    for d in range(1, inner):
        remote(ids_all.at[inner_at], ids_all.at[inner_at], ids_send.at[d], ids_recv.at[d], {"row": place(0, d)})
    per_bands = bands // CHUNKS
    for c in range(CHUNKS):
        for b in range(c * per_bands, (c + 1) * per_bands):
            tile_copies[b].wait()
        transposed(0, dual_ref, c * per_bands, per_bands)
        send_chunk(0, c)
    for d in range(1, inner):
        await_recv(ids_all.at[lax.rem(inner_at + inner - d, inner)], ids_recv.at[d])
    for src in range(inner):
        build_hot(src)
    index = lax.broadcasted_iota(jnp.int32, (local, blocks), 1)
    hot_own[...] = jnp.where(index == ids_col[...], 1.0, 0.0).astype(jnp.bfloat16)
    for copy in in_copies:
        copy.wait()
    partial[0, col, 8:16, :] = primal_update(0, step_size)
    spread_finish(0)
    forward(0)
    send_partials(0)
    total = sum_partials(0)
    dual = dual_ref[...]
    dual_one = project_dual(dual + step_size * (right_ref[...] - total[:bands]), row_kinds_ref[...])
    dual_out[...] = dual_one
    moved[row, :bands, :] = (dual_one - dual) ** 2
    moved[row, bands:, :] = total[8:16]

    for c in range(CHUNKS):
        transposed(1, dual_out, c * per_bands, per_bands)
        send_chunk(1, c)
        if c == 0:
            for d in range(1, rows):
                remote(moved.at[row], moved.at[row], mov_send.at[d], mov_recv.at[d],
                       {"row": lax.rem(row + d, rows)})
    for d in range(1, rows):
        await_recv(moved.at[lax.rem(row + rows - d, rows)], mov_recv.at[d])
    squares = moved[0]
    for r in range(1, rows):
        squares = squares + moved[r]
    dual_moved = jnp.sum(squares[:bands], keepdims=True)
    primal_moved = jnp.sum(squares[bands:], keepdims=True)
    weight = jnp.sqrt(jnp.sqrt((dual_moved + epsilon) / (primal_moved + epsilon)))
    primal_update(1, step_size / weight)
    partial[1, col, 8:16, :] = jnp.zeros((8, width), jnp.float32)
    spread_finish(1)
    forward(1)
    send_partials(1)
    spread_finish(2)
    out_copy = pltpu.make_async_copy(result, primal_out, out_sem)
    out_copy.start()
    total = sum_partials(1)
    dual_out[...] = project_dual(
        dual_one + (step_size * weight) * (right_ref[...] - total[:bands]), row_kinds_ref[...]
    )
    for copy in pending:
        copy.wait_send()
    out_copy.wait()


def per_device(
    rows, cols,
    tile_values, block_cols, primal_start, dual_start, cost_vector,
    lower_bound, upper_bound, var_kinds, right_side, row_kinds,
):
    bands, slots, width, _ = tile_values.shape
    blocks = primal_start.shape[0] // width
    local = bands * slots
    inner = rows // OUTER
    ids = block_cols - lax.axis_index("col") * blocks
    vmem = pl.BlockSpec(memory_space=pltpu.VMEM)
    hbm = pl.BlockSpec(memory_space=pl.ANY)
    dma = pltpu.SemaphoreType.DMA
    tall = (blocks, width)
    short = (blocks // rows, width)
    primal_final, dual_final = pl.pallas_call(
        functools.partial(kernel, rows, cols, bands, slots, width, blocks),
        out_shape=(
            jax.ShapeDtypeStruct(tall, jnp.float32),
            jax.ShapeDtypeStruct((bands, width), jnp.float32),
        ),
        in_specs=[hbm, vmem, vmem] + [hbm] * 5 + [vmem] * 3,
        out_specs=(hbm, vmem),
        scratch_shapes=[
            pltpu.VMEM((bands, slots, width, width), jnp.bfloat16),
            pltpu.VMEM(short, jnp.float32),
            pltpu.VMEM(short, jnp.float32),
            pltpu.VMEM(short, jnp.float32),
            pltpu.VMEM(short, jnp.float32),
            pltpu.VMEM(short, jnp.int32),
            pltpu.VMEM(short, jnp.float32),
            pltpu.VMEM(tall, jnp.float32),
            pltpu.VMEM((inner, blocks // inner, local), jnp.bfloat16),
            pltpu.VMEM((local, blocks), jnp.bfloat16),
            pltpu.VMEM((2,) + tall, jnp.bfloat16),
            pltpu.VMEM((local, width), jnp.bfloat16),
            pltpu.VMEM((2, inner, local, 2 * width), jnp.bfloat16),
            pltpu.VMEM((inner, 1, local), jnp.int32),
            pltpu.VMEM((2, OUTER) + short, jnp.float32),
            pltpu.VMEM((2, OUTER) + short, jnp.float32),
            pltpu.VMEM((2, cols, 16, width), jnp.float32),
            pltpu.VMEM((rows, bands + 8, width), jnp.float32),
            dma((bands,)),
            dma((5,)),
            dma,
            dma((2, inner, CHUNKS)),
            dma((2, inner, CHUNKS)),
            dma((2, OUTER)),
            dma((2, OUTER)),
            dma((3, OUTER, inner)),
            dma((3, OUTER, inner)),
            dma((3, OUTER, inner)),
            dma((inner,)),
            dma((inner,)),
            dma((2, cols)),
            dma((2, cols)),
            dma((rows,)),
            dma((rows,)),
        ],
        compiler_params=pltpu.CompilerParams(
            collective_id=0, has_side_effects=True, vmem_limit_bytes=56 * 1024 * 1024
        ),
    )(
        tile_values,
        ids.reshape(1, local),
        ids.reshape(local, 1),
        primal_start.reshape(tall),
        cost_vector.reshape(tall),
        lower_bound.reshape(tall),
        upper_bound.reshape(tall),
        var_kinds.reshape(tall),
        dual_start.reshape(bands, width),
        right_side.reshape(bands, width),
        row_kinds.reshape(bands, width),
    )
    return primal_final.reshape(-1), dual_final.reshape(-1)


def solution(mesh):
    return jax.shard_map(
        functools.partial(per_device, mesh.shape["row"], mesh.shape["col"]),
        mesh=mesh,
        in_specs=(
            P("row", "col", None, None),
            P("row", "col"),
            P("col"),
            P("row"),
            P("col"),
            P("col"),
            P("col"),
            P("col"),
            P("row"),
            P("row"),
        ),
        out_specs=(P("col"), P("row")),
        check_vma=False,
    )
```
